768 devices in a mesh: fsdp: 32 (over y, x_hi, core), tensor: 24 (over x_lo, z).
Axes of the slice: x: 4 (x_hi: 2, x_lo: 2; x = x_hi * 2 + x_lo), y: 8, z: 12, core: 2. Of those that a mesh axis runs over, the one named last changes fastest.
Arguments:
- tokens: bfloat16 [6144, 4096], P('fsdp'), may hold values from -80 to 80
- norm_gain: float32 [4096], P('fsdp'), may hold values from 0.25 to 1.75
- gate_weight: bfloat16 [4096, 15360], P('fsdp', 'tensor'), may hold values from -0.09375 to 0.09375
- up_weight: bfloat16 [4096, 15360], P('fsdp', 'tensor'), may hold values from -0.09375 to 0.09375
Outputs:
- hidden: bfloat16 [6144, 15360], P('fsdp', 'tensor')
The draws below stay inside these ranges and needn't reach their ends.
All inputs are finite; a program needn't handle non-finite values.
Results may differ from the reference program's by a relative error of at most 0.0058.
Values may be sent and summed in bfloat16 or wider, within the bound.
No kernel may reach another device: no remote copies, remote signals or barrier semaphores. Data moves between devices by JAX's collectives and lax.ppermute only.
A program may use at most 32 MiB of HBM per device.

```python
import math
import jax
import jax.numpy as jnp
from jax import lax

D = 4096
TOKENS = 6144
FF = 15360


def draw_tokens(key, part):
    key = jax.random.fold_in(key, 11)
    key_base, key_rows, key_cols = jax.random.split(key, 3)
    base = jax.random.normal(key_base, (TOKENS, D), jnp.float32)
    rows = jnp.exp(jax.random.uniform(key_rows, (TOKENS, 1), jnp.float32, 0.0, math.log(10.0)))
    columns = jnp.exp(jax.random.uniform(key_cols, (1, D), jnp.float32, 0.0, math.log(10.0)))
    return jnp.clip(0.1 * base * rows * columns, -80.0, 80.0).astype(jnp.bfloat16)


def shard_levels(own_key, shape, cuts, least, top_value):
    factor_of = 1.0
    for dim, shards_of in cuts:
        draws = jax.random.uniform(jax.random.fold_in(jax.random.fold_in(own_key, 6), dim), (shards_of,), jnp.float32, least / len(cuts), top_value / len(cuts))
        factor_of = factor_of * jnp.repeat(jnp.exp(draws), shape[dim] // shards_of).reshape((-1,) + (1,) * (len(shape) - 1 - dim))
    return factor_of


def noise(rng, dims, scale, most, cuts=(), dtype=jnp.bfloat16):
    result = jax.random.normal(rng, dims, jnp.float32) * scale
    if len(cuts) > 0:
        result = shard_levels(rng, dims, cuts, -0.22, 0.18) * result
    return jnp.clip(result, min=-most, max=most).astype(dtype)


def setup_inputs(seed: int = 0) -> dict:
    key_of = jax.random.split(jax.random.key(seed), 5)
    return {
        "tokens": draw_tokens(jax.random.fold_in(key_of[4], 71), 0),
        "norm_gain": jnp.clip(1.0 + 0.15 * jax.random.normal(key_of[1], (D,), jnp.float32), 0.25, 1.75),
        "gate_weight": noise(key_of[2], (D, FF), D ** -0.5, 0.09375, ((0, 32), (1, 24))),
        "up_weight": noise(key_of[3], (D, FF), D ** -0.5, 0.09375, ((0, 32), (1, 24))),
    }


epsilon = 1e-05

def reference(tokens, norm_gain, gate_weight, up_weight):
    values = tokens.astype(jnp.float32)
    row_scale = lax.rsqrt(lax.optimization_barrier(jnp.mean(values * values, axis=1, keepdims=True)) + epsilon)
    normed = (values * row_scale * norm_gain[None, :]).astype(jnp.bfloat16)
    gate = jnp.dot(normed, gate_weight, preferred_element_type=jnp.float32)
    up = jnp.dot(normed, up_weight, preferred_element_type=jnp.float32)
    return (jax.nn.silu(gate) * up).astype(jnp.bfloat16)
```

```python
import functools

import jax
import jax.numpy as jnp
import numpy as np
from jax import lax
from jax.experimental import pallas as pl
from jax.experimental.pallas import tpu as pltpu
from jax.sharding import PartitionSpec as P

epsilon = 1e-05
vmem_bytes = 40 * 1024 * 1024


def load_blocks(blocks, held, sems):
    copies = [pltpu.make_async_copy(b, held.at[i], sems.at[i]) for i, b in enumerate(blocks)]
    for copy in copies:
        copy.start()
    return copies


def add_blocks(places, tokens, held, copies, total):
    depth = held.shape[1]
    for i, copy in enumerate(copies):
        copy.wait()
        start = pl.multiple_of(places[i] * depth, depth)
        total[...] += jnp.dot(tokens[:, pl.ds(start, depth)], held[i], preferred_element_type=jnp.float32)


def first_kernel(n, places, tokens, *refs):
    blocks, (total, scale, held, sems) = refs[:n], refs[n:]
    copies = load_blocks(blocks, held, sems)
    values = tokens[...].astype(jnp.float32)
    scale[...] = lax.rsqrt(jnp.mean(values * values, axis=1, keepdims=True) + epsilon)
    total[...] = jnp.zeros_like(total)
    add_blocks(places, tokens, held, copies, total)


def next_kernel(n, places, tokens, before, *refs):
    blocks, (total, held, sems) = refs[:n], refs[n:]
    copies = load_blocks(blocks, held, sems)
    total[...] = before[...]
    add_blocks(places, tokens, held, copies, total)


def last_kernel(n, places, tokens, before, scale, *refs):
    blocks, (hidden, total, held, sems) = refs[:n], refs[n:]
    copies = load_blocks(blocks, held, sems)
    total[...] = before[...]
    add_blocks(places, tokens, held, copies, total)
    wide = hidden.shape[1]
    gate = total[:, :wide] * scale[...]
    up = total[:, wide:] * scale[...]
    hidden[...] = (gate / (1.0 + jnp.exp(-gate)) * up).astype(hidden.dtype)


def call(kernel, places, tokens, extra, blocks, out_shape, out_specs, scratch):
    n = len(blocks)
    depth, wide = blocks[0].shape
    rows = tokens.shape[0]
    vmem = pl.BlockSpec(memory_space=pltpu.VMEM)
    return pl.pallas_call(
        functools.partial(kernel, n),
        out_shape=out_shape,
        in_specs=[pl.BlockSpec(memory_space=pltpu.SMEM)] + [vmem] * (1 + len(extra)) + [pl.BlockSpec(memory_space=pl.ANY)] * n,
        out_specs=out_specs,
        scratch_shapes=scratch + [pltpu.VMEM((n, depth, wide), blocks[0].dtype), pltpu.SemaphoreType.DMA((n,))],
        compiler_params=pltpu.CompilerParams(vmem_limit_bytes=vmem_bytes),
        cost_estimate=pl.CostEstimate(
            flops=2 * n * rows * depth * wide, bytes_accessed=2 * n * depth * wide + 4 * rows * wide, transcendentals=0
        ),
    )(places, tokens, *extra, *blocks)


def make_on_device(count):
    high = count // 4

    def move(where):
        pairs = []
        for f in range(count):
            y, x, c = where(f // 4, (f // 2) % 2, f % 2)
            pairs.append((f, (y % high) * 4 + (x % 2) * 2 + c % 2))
        return lambda v: lax.ppermute(v, "fsdp", pairs)

    along = move(lambda y, x, c: (y + 1 - 2 * c, x, c))
    slant = move(lambda y, x, c: (y + 1 - 2 * c, x + 1, c))
    across = move(lambda y, x, c: (y, x + 1, c))
    swap = move(lambda y, x, c: (y, x, c + 1))
    core_pairs = [[f, f + 1] for f in range(0, count, 2)]

    def place(f, steps, other):
        y, x, c = f // 4, (f // 2) % 2, f % 2
        return (y + steps * (2 * c - 1)) % high * 2 + (x + other) % 2

    def places(index, *which):
        table = np.array([[place(f, *w) for w in which] for f in range(count)], np.int32)
        return lax.dynamic_index_in_dim(jnp.asarray(table), index, 0, keepdims=False)

    def join(v):
        return lax.all_gather(v, "fsdp", axis=0, tiled=True, axis_index_groups=core_pairs)

    def on_device(tokens, norm_gain, gate_weight, up_weight):
        index = lax.axis_index("fsdp")
        c = lax.bitwise_and(index, 1)
        gain = norm_gain[:, None]
        own = jnp.concatenate([gate_weight * gain, up_weight * gain], axis=1).astype(jnp.bfloat16)
        depth, wide = own.shape
        chip = join(own)

        a1, b1 = along(chip), slant(chip)
        a2, b2 = along(a1), along(b1)
        a3, b3 = along(a2), along(b2)
        a4 = along(lax.dynamic_slice_in_dim(a3, c * depth, depth, 0))
        b4 = along(lax.dynamic_slice_in_dim(b3, c * depth, depth, 0))
        b0 = across(chip)

        rows = tokens.shape[0]
        sums = jax.ShapeDtypeStruct((rows, wide), jnp.float32)
        vmem = pl.BlockSpec(memory_space=pltpu.VMEM)
        total, scale = call(
            first_kernel,
            places(index, (0, 0), (1, 0), (-1, 0), (1, 1), (-1, 1), (2, 0), (-2, 0)),
            tokens,
            [],
            [chip, a1, swap(a1), b1, swap(b1), a2, swap(a2)],
            (sums, jax.ShapeDtypeStruct((rows, 1), jnp.float32)),
            (vmem, vmem),
            [],
        )
        total = call(
            next_kernel,
            places(index, (0, 1), (2, 1), (-2, 1), (3, 0), (-3, 0), (3, 1), (-3, 1)),
            tokens,
            [total],
            [b0, b2, swap(b2), a3, swap(a3), b3, swap(b3)],
            sums,
            vmem,
            [],
        )
        a4, total = lax.optimization_barrier((a4, total))
        return call(
            last_kernel,
            places(index, (4, 0), (4, 1)),
            tokens,
            [total, scale],
            [join(a4), join(b4)],
            jax.ShapeDtypeStruct((rows, wide // 2), jnp.bfloat16),
            vmem,
            [pltpu.VMEM((rows, wide), jnp.float32)],
        )

    return on_device


def solution(mesh):
    return jax.shard_map(
        make_on_device(mesh.shape["fsdp"]),
        mesh=mesh,
        in_specs=(P("fsdp", None), P("fsdp"), P("fsdp", "tensor"), P("fsdp", "tensor")),
        out_specs=P("fsdp", "tensor"),
        check_vma=False,
    )
```

```python
import functools

import jax
import jax.numpy as jnp
import numpy as np
from jax import lax
from jax.experimental import pallas as pl
from jax.experimental.pallas import tpu as pltpu
from jax.sharding import PartitionSpec as P

epsilon = 1e-05
vmem_bytes = 40 * 1024 * 1024
unit, piece = 128, 256


def pieces(blocks):
    return [(b, at, min(piece, b.shape[0])) for b in blocks for at in range(0, b.shape[0], piece)]


def load_blocks(blocks, held, sems):
    copies, to = [], 0
    for i, (block, at, depth) in enumerate(pieces(blocks)):
        rows = pl.ds(to, depth)
        copies.append((pltpu.make_async_copy(block.at[pl.ds(at, depth)], held.at[rows], sems.at[i]), rows))
        to += depth
    for copy, _ in copies:
        copy.start()
    return copies


def add_blocks(places, held, copies, pairs):
    for i, (copy, rows) in enumerate(copies):
        copy.wait()
        start = pl.multiple_of(places[i] * unit, unit)
        for tokens, total in pairs:
            total[...] += jnp.dot(tokens[:, pl.ds(start, rows.size)], held[rows], preferred_element_type=jnp.float32)


def first_kernel(n, places, tokens, others, *refs):
    blocks, (total, partial, scale, held, sems) = refs[:n], refs[n:]
    copies = load_blocks(blocks, held, sems)
    values = tokens[...].astype(jnp.float32)
    scale[...] = lax.rsqrt(jnp.mean(values * values, axis=1, keepdims=True) + epsilon)
    total[...] = jnp.zeros_like(total)
    partial[...] = jnp.zeros_like(partial)
    add_blocks(places, held, copies, [(tokens, total), (others, partial)])


def next_kernel(n, places, tokens, others, total_before, partial_before, *refs):
    blocks, (total, partial, held, sems) = refs[:n], refs[n:]
    copies = load_blocks(blocks, held, sems)
    total[...] = total_before[...]
    partial[...] = partial_before[...]
    add_blocks(places, held, copies, [(tokens, total), (others, partial)])


def last_kernel(n, places, tokens, total_before, partial_arrived, scale, *refs):
    blocks, (hidden, total, held, sems) = refs[:n], refs[n:]
    copies = load_blocks(blocks, held, sems)
    total[...] = total_before[...] + partial_arrived[...]
    add_blocks(places, held, copies, [(tokens, total)])
    wide = hidden.shape[1]
    gate = total[:, :wide] * scale[...]
    up = total[:, wide:] * scale[...]
    hidden[...] = (gate / (1.0 + jnp.exp(-gate)) * up).astype(hidden.dtype)


def call(kernel, places, arrays, blocks, out_shape, scratch=()):
    n = len(blocks)
    depth, wide = sum(b.shape[0] for b in blocks), blocks[0].shape[1]
    rows = arrays[0].shape[0]
    vmem = pl.BlockSpec(memory_space=pltpu.VMEM)
    return pl.pallas_call(
        functools.partial(kernel, n),
        out_shape=out_shape,
        in_specs=[pl.BlockSpec(memory_space=pltpu.SMEM)] + [vmem] * len(arrays) + [pl.BlockSpec(memory_space=pl.ANY)] * n,
        out_specs=jax.tree.map(lambda _: vmem, out_shape),
        scratch_shapes=list(scratch) + [pltpu.VMEM((depth, wide), blocks[0].dtype), pltpu.SemaphoreType.DMA((len(pieces(blocks)),))],
        compiler_params=pltpu.CompilerParams(vmem_limit_bytes=vmem_bytes),
        cost_estimate=pl.CostEstimate(
            flops=4 * rows * depth * wide, bytes_accessed=2 * depth * wide + 16 * rows * wide, transcendentals=0
        ),
    )(places, *arrays, *blocks)


def make_on_device(count):
    high = count // 4

    def move(where):
        pairs = []
        for f in range(count):
            y, x, c = where(f // 4, (f // 2) % 2, f % 2)
            pairs.append((f, (y % high) * 4 + (x % 2) * 2 + c % 2))
        return lambda v: lax.ppermute(v, "fsdp", pairs)

    along = move(lambda y, x, c: (y + 1 - 2 * c, x, c))
    slant = move(lambda y, x, c: (y + 1 - 2 * c, x + 1, c))
    across = move(lambda y, x, c: (y, x + 1, c))
    swap = move(lambda y, x, c: (y, x, c + 1))
    core_pairs = [[f, f + 1] for f in range(0, count, 2)]

    def place(f, steps, other, half=False):
        y, x, c = f // 4, (f // 2) % 2, f % 2
        return ((y + steps * (2 * c - 1)) % high * 2 + (x + other) % 2) * 2 + (c if half else 0)

    def places(index, *which):
        table = np.array([[place(f, *w) for w in which] for f in range(count)], np.int32)
        return lax.dynamic_index_in_dim(jnp.asarray(table), index, 0, keepdims=False)

    def join(v):
        return lax.all_gather(v, "fsdp", axis=0, tiled=True, axis_index_groups=core_pairs)

    def on_device(tokens, norm_gain, gate_weight, up_weight):
        index = lax.axis_index("fsdp")
        gain = norm_gain[:, None]
        own = jnp.concatenate([gate_weight * gain, up_weight * gain], axis=1).astype(jnp.bfloat16)
        depth, wide = own.shape
        half = lax.bitwise_and(index, 1) * depth
        chip, late = lax.optimization_barrier((join(own), tokens))

        rows = tokens.shape[0]
        sums = jax.ShapeDtypeStruct((rows, wide), jnp.float32)

        a1 = along(chip)
        b1 = slant(chip)
        others = swap(late)
        b0 = across(own)
        a2 = along(a1)
        b2 = along(b1)
        a3 = along(a2)
        total, partial, scale = call(
            first_kernel,
            places(index, (0, 0, True), (0, 1, True), (1, 0), (1, 1), (2, 0)),
            [tokens, others],
            [own, b0, a1, b1, a2],
            (sums, sums, jax.ShapeDtypeStruct((rows, 1), jnp.float32)),
        )
        b2, total = lax.optimization_barrier((b2, total))
        b3 = along(b2)
        a4 = along(lax.dynamic_slice_in_dim(a3, half, depth, 0))
        total, partial = call(
            next_kernel,
            places(index, (2, 1), (3, 0)),
            [tokens, others, total, partial],
            [b2, a3],
            (sums, sums),
        )
        b3, total = lax.optimization_barrier((b3, total))
        b4 = along(lax.dynamic_slice_in_dim(b3, half, depth, 0))
        return call(
            last_kernel,
            places(index, (3, 1), (-3, 1), (4, 0), (4, 1)),
            [tokens, total, swap(partial), scale],
            [b3, swap(b3), join(a4), join(b4)],
            jax.ShapeDtypeStruct((rows, wide // 2), jnp.bfloat16),
            [pltpu.VMEM((rows, wide), jnp.float32)],
        )

    return on_device


def solution(mesh):
    return jax.shard_map(
        make_on_device(mesh.shape["fsdp"]),
        mesh=mesh,
        in_specs=(P("fsdp", None), P("fsdp"), P("fsdp", "tensor"), P("fsdp", "tensor")),
        out_specs=P("fsdp", "tensor"),
        check_vma=False,
    )
```

```python
import functools

import jax
import jax.numpy as jnp
from jax import lax
from jax.experimental import pallas as pl
from jax.experimental.pallas import tpu as pltpu
from jax.sharding import PartitionSpec as P

epsilon = 1e-05
vmem_bytes = 16 * 1024 * 1024


def column(spec, high):
    steps, other, half = spec
    index = lax.axis_index("fsdp")
    core = lax.rem(index, 2)
    x = lax.rem(lax.div(index, 2), 2)
    y = lax.rem(lax.div(index, 4) + (steps * (2 * core - 1) + high), high)
    return (y * 2 + (1 - x if other else x)) * 2 + (core if half else 0)


def add_blocks(specs, high, blocks, pairs):
    for spec, block in zip(specs, blocks):
        depth = block.shape[0]
        unit = depth if spec[2] else depth // 2
        start = pl.multiple_of(column(spec, high) * unit, unit)
        for tokens, total in pairs:
            total[...] += jnp.dot(tokens[:, pl.ds(start, depth)], block[...], preferred_element_type=jnp.float32)


def first_kernel(add, n, tokens, others, *refs):
    blocks, (total, partial, scale) = refs[:n], refs[n:]
    values = tokens[...].astype(jnp.float32)
    scale[...] = lax.rsqrt(jnp.mean(values * values, axis=1, keepdims=True) + epsilon)
    total[...] = jnp.zeros_like(total)
    partial[...] = jnp.zeros_like(partial)
    add(blocks, [(tokens, total), (others, partial)])


def second_kernel(add, n, tokens, others, total_before, partial_before, *refs):
    blocks, (total, partial) = refs[:n], refs[n:]
    total[...] = total_before[...]
    partial[...] = partial_before[...]
    add(blocks, [(tokens, total), (others, partial)])


def third_kernel(add, n, tokens, total_before, partial_arrived, *refs):
    blocks, (total,) = refs[:n], refs[n:]
    total[...] = total_before[...] + partial_arrived[...]
    add(blocks, [(tokens, total)])


def last_kernel(add, n, tokens, total_before, scale, *refs):
    blocks, (hidden, total) = refs[:n], refs[n:]
    total[...] = total_before[...]
    add(blocks, [(tokens, total)])
    wide = hidden.shape[1]
    gate = total[:, :wide] * scale[...]
    up = total[:, wide:] * scale[...]
    hidden[...] = (gate / (1.0 + jnp.exp(-gate)) * up).astype(hidden.dtype)


def call(kernel, *, high, specs, arrays, blocks, out_shape, scratch=()):
    n = len(blocks)
    depth, wide = sum(b.shape[0] for b in blocks), blocks[0].shape[1]
    rows = arrays[0].shape[0]
    vmem = pl.BlockSpec(memory_space=pltpu.VMEM)
    return pl.pallas_call(
        functools.partial(kernel, functools.partial(add_blocks, specs, high), n),
        out_shape=out_shape,
        in_specs=[vmem] * (len(arrays) + n),
        out_specs=jax.tree.map(lambda _: vmem, out_shape),
        scratch_shapes=list(scratch),
        compiler_params=pltpu.CompilerParams(vmem_limit_bytes=vmem_bytes),
        cost_estimate=pl.CostEstimate(
            flops=4 * rows * depth * wide, bytes_accessed=2 * depth * wide + 16 * rows * wide, transcendentals=0
        ),
    )(*arrays, *blocks)


def make_on_device(count):
    high = count // 4

    def move(where):
        pairs = []
        for f in range(count):
            y, x, c = where(f // 4, (f // 2) % 2, f % 2)
            pairs.append((f, (y % high) * 4 + (x % 2) * 2 + c % 2))
        return lambda v: lax.ppermute(v, "fsdp", pairs)

    along = move(lambda y, x, c: (y + 1 - 2 * c, x, c))
    slant = move(lambda y, x, c: (y + 1 - 2 * c, x + 1, c))
    across = move(lambda y, x, c: (y, x + 1, c))
    swap = move(lambda y, x, c: (y, x, c + 1))
    core_pairs = [[f, f + 1] for f in range(0, count, 2)]

    def join(v):
        return lax.all_gather(v, "fsdp", axis=0, tiled=True, axis_index_groups=core_pairs)

    def on_device(tokens, norm_gain, gate_weight, up_weight):
        index = lax.axis_index("fsdp")
        gain = norm_gain[:, None]
        own = jnp.concatenate([gate_weight * gain, up_weight * gain], axis=1).astype(jnp.bfloat16)
        depth, wide = own.shape
        half = lax.bitwise_and(index, 1) * depth
        chip = join(own)
        rows = tokens.shape[0]
        sums = jax.ShapeDtypeStruct((rows, wide), jnp.float32)
        step = functools.partial(call, high=high)

        late0 = tokens
        a1 = along(chip)
        b1 = slant(chip)
        others = swap(late0)
        a2 = along(a1)
        b2 = along(b1)
        a3 = along(a2)
        total, partial, scale = step(
            first_kernel,
            specs=[(0, 0, 1), (1, 0, 0), (1, 1, 0), (2, 0, 0)],
            arrays=[tokens, others],
            blocks=[own, a1, b1, a2],
            out_shape=(sums, sums, jax.ShapeDtypeStruct((rows, 1), jnp.float32)),
        )
        b2, total = lax.optimization_barrier((b2, total))
        b2, chip = lax.optimization_barrier((b2, chip))
        b0 = across(chip)
        b3 = along(b2)
        a4 = along(lax.dynamic_slice_in_dim(a3, half, depth, 0))
        total, partial = step(
            second_kernel,
            specs=[(2, 1, 0), (3, 0, 0)],
            arrays=[tokens, others, total, partial],
            blocks=[b2, a3],
            out_shape=(sums, sums),
        )
        b3, total = lax.optimization_barrier((b3, total))
        bs = lax.dynamic_slice_in_dim(b3, half, depth, 0)
        b4 = along(bs)
        a4, late = lax.optimization_barrier((a4, b3))
        partial = swap(partial)
        total = step(
            third_kernel,
            specs=[(0, 1, 0), (3, 1, 0), (-3, 1, 0), (4, 0, 0)],
            arrays=[tokens, total, partial],
            blocks=[b0, b3, swap(late), join(a4)],
            out_shape=sums,
        )
        b4, total = lax.optimization_barrier((b4, total))
        return step(
            last_kernel,
            specs=[(4, 1, 0)],
            arrays=[tokens, total, scale],
            blocks=[join(b4)],
            out_shape=jax.ShapeDtypeStruct((rows, wide // 2), jnp.bfloat16),
            scratch=[pltpu.VMEM((rows, wide), jnp.float32)],
        )

    return on_device


def solution(mesh):
    return jax.shard_map(
        make_on_device(mesh.shape["fsdp"]),
        mesh=mesh,
        in_specs=(P("fsdp", None), P("fsdp"), P("fsdp", "tensor"), P("fsdp", "tensor")),
        out_specs=P("fsdp", "tensor"),
        check_vma=False,
    )
```

```python
import functools

import jax
import jax.numpy as jnp
from jax import lax
from jax.experimental import pallas as pl
from jax.experimental.pallas import tpu as pltpu
from jax.sharding import PartitionSpec as P

epsilon = 1e-05
vmem_bytes = 16 * 1024 * 1024


def column(spec, high):
    steps, other, half = spec
    index = lax.axis_index("fsdp")
    core = lax.rem(index, 2)
    x = lax.rem(lax.div(index, 2), 2)
    y = lax.rem(lax.div(index, 4) + (steps * (2 * core - 1) + high), high)
    return (y * 2 + (1 - x if other else x)) * 2 + (core if half else 0)


def add_blocks(specs, high, blocks, pairs):
    for spec, block in zip(specs, blocks):
        depth = block.shape[0]
        unit = depth if spec[2] else depth // 2
        start = pl.multiple_of(column(spec, high) * unit, unit)
        for tokens, total in pairs:
            total[...] += jnp.dot(tokens[:, pl.ds(start, depth)], block[...], preferred_element_type=jnp.float32)


def first_kernel(add, n, tokens, others, *refs):
    blocks, (total, partial, scale) = refs[:n], refs[n:]
    values = tokens[...].astype(jnp.float32)
    scale[...] = lax.rsqrt(jnp.mean(values * values, axis=1, keepdims=True) + epsilon)
    total[...] = jnp.zeros_like(total)
    partial[...] = jnp.zeros_like(partial)
    add(blocks, [(tokens, total), (others, partial)])


def second_kernel(add, n, tokens, others, total_before, partial_before, *refs):
    blocks, (total, partial) = refs[:n], refs[n:]
    total[...] = total_before[...]
    partial[...] = partial_before[...]
    add(blocks, [(tokens, total), (others, partial)])


def third_kernel(add, n, tokens, others, total_before, partial_before, *refs):
    blocks, (total, gate, up, sums) = refs[:n], refs[n:]
    total[...] = total_before[...]
    sums[...] = partial_before[...]
    add(blocks, [(tokens, total), (others, sums)])
    wide = gate.shape[1]
    gate[...] = sums[:, :wide]
    up[...] = sums[:, wide:]


def last_kernel(add, n, tokens, total_before, gate_arrived, up_arrived, scale, *refs):
    blocks, (hidden, total) = refs[:n], refs[n:]
    rows, wide = hidden.shape
    theirs = pl.ds(pl.multiple_of((1 - lax.rem(lax.axis_index("fsdp"), 2)) * rows, rows), rows)
    total[:, :wide] = total_before[:, :wide] + gate_arrived[theirs, :]
    total[:, wide:] = total_before[:, wide:] + up_arrived[theirs, :]
    add(blocks, [(tokens, total)])
    gate = total[:, :wide] * scale[...]
    up = total[:, wide:] * scale[...]
    hidden[...] = (gate / (1.0 + jnp.exp(-gate)) * up).astype(hidden.dtype)


def call(kernel, *, high, specs, arrays, blocks, out_shape, scratch=()):
    n = len(blocks)
    depth, wide = sum(b.shape[0] for b in blocks), blocks[0].shape[1]
    rows = arrays[0].shape[0]
    vmem = pl.BlockSpec(memory_space=pltpu.VMEM)
    return pl.pallas_call(
        functools.partial(kernel, functools.partial(add_blocks, specs, high), n),
        out_shape=out_shape,
        in_specs=[vmem] * (len(arrays) + n),
        out_specs=jax.tree.map(lambda _: vmem, out_shape),
        scratch_shapes=list(scratch),
        compiler_params=pltpu.CompilerParams(vmem_limit_bytes=vmem_bytes),
        cost_estimate=pl.CostEstimate(
            flops=4 * rows * depth * wide, bytes_accessed=2 * depth * wide + 16 * rows * wide, transcendentals=0
        ),
    )(*arrays, *blocks)


def make_on_device(count):
    high = count // 4

    def move(where):
        pairs = []
        for f in range(count):
            y, x, c = where(f // 4, (f // 2) % 2, f % 2)
            pairs.append((f, (y % high) * 4 + (x % 2) * 2 + c % 2))
        return lambda v: lax.ppermute(v, "fsdp", pairs)

    along = move(lambda y, x, c: (y + 1 - 2 * c, x, c))
    slant = move(lambda y, x, c: (y + 1 - 2 * c, x + 1, c))
    across = move(lambda y, x, c: (y, x + 1, c))
    swap = move(lambda y, x, c: (y, x, c + 1))
    core_pairs = [[f, f + 1] for f in range(0, count, 2)]

    def join(v):
        return lax.all_gather(v, "fsdp", axis=0, tiled=True, axis_index_groups=core_pairs)

    def on_device(tokens, norm_gain, gate_weight, up_weight):
        index = lax.axis_index("fsdp")
        gain = norm_gain[:, None]
        own = jnp.concatenate([gate_weight * gain, up_weight * gain], axis=1).astype(jnp.bfloat16)
        depth, wide = own.shape
        half = lax.bitwise_and(index, 1) * depth
        chip = join(own)
        rows = tokens.shape[0]
        sums = jax.ShapeDtypeStruct((rows, wide), jnp.float32)
        step = functools.partial(call, high=high)

        a1 = along(chip)
        b1 = slant(chip)
        others = swap(tokens)
        a2 = along(a1)
        b2 = along(b1)
        a3 = along(a2)
        total, partial, scale = step(
            first_kernel,
            specs=[(0, 0, 1), (1, 0, 0), (1, 1, 0), (2, 0, 0)],
            arrays=[tokens, others],
            blocks=[own, a1, b1, a2],
            out_shape=(sums, sums, jax.ShapeDtypeStruct((rows, 1), jnp.float32)),
        )
        b2, total, late = lax.optimization_barrier((b2, total, own))
        b3 = along(b2)
        a4 = along(lax.dynamic_slice_in_dim(a3, half, depth, 0))
        b0 = across(late)
        total, partial = step(
            second_kernel,
            specs=[(0, 1, 1), (2, 1, 0), (3, 0, 0)],
            arrays=[tokens, others, total, partial],
            blocks=[b0, b2, a3],
            out_shape=(sums, sums),
        )
        b3, total = lax.optimization_barrier((b3, total))
        b4 = along(lax.dynamic_slice_in_dim(b3, half, depth, 0))
        narrow = jax.ShapeDtypeStruct((rows, wide // 2), jnp.float32)
        total, *partial = step(
            third_kernel,
            specs=[(3, 1, 0), (4, 0, 1)],
            arrays=[tokens, others, total, partial],
            blocks=[b3, a4],
            out_shape=(sums, narrow, narrow),
            scratch=[pltpu.VMEM((rows, wide), jnp.float32)],
        )
        partial = [join(v) for v in partial]
        return step(
            last_kernel,
            specs=[(4, 1, 0)],
            arrays=[tokens, total, *partial, scale],
            blocks=[join(b4)],
            out_shape=jax.ShapeDtypeStruct((rows, wide // 2), jnp.bfloat16),
            scratch=[pltpu.VMEM((rows, wide), jnp.float32)],
        )

    return on_device


def solution(mesh):
    return jax.shard_map(
        make_on_device(mesh.shape["fsdp"]),
        mesh=mesh,
        in_specs=(P("fsdp", None), P("fsdp"), P("fsdp", "tensor"), P("fsdp", "tensor")),
        out_specs=P("fsdp", "tensor"),
        check_vma=False,
    )
```

```python
import functools

import jax
import jax.numpy as jnp
from jax import lax
from jax.experimental import pallas as pl
from jax.experimental.pallas import tpu as pltpu
from jax.sharding import PartitionSpec as P

epsilon = 1e-05
vmem_bytes = 16 * 1024 * 1024


def column(spec, high):
    steps, other, half = spec
    index = lax.axis_index("fsdp")
    core = lax.rem(index, 2)
    x = lax.rem(lax.div(index, 2), 2)
    y = lax.rem(lax.div(index, 4) + (steps * (2 * core - 1) + high), high)
    return (y * 2 + (1 - x if other else x)) * 2 + (core if half else 0)


def add_blocks(specs, high, blocks, pairs):
    for spec, block in zip(specs, blocks):
        depth = block.shape[0]
        unit = depth if spec[2] else depth // 2
        start = pl.multiple_of(column(spec, high) * unit, unit)
        for tokens, total in pairs:
            total[...] += jnp.dot(tokens[:, pl.ds(start, depth)], block[...], preferred_element_type=jnp.float32)


def first_kernel(add, n, tokens, others, *refs):
    blocks, (total, partial, scale) = refs[:n], refs[n:]
    values = tokens[...].astype(jnp.float32)
    scale[...] = lax.rsqrt(jnp.mean(values * values, axis=1, keepdims=True) + epsilon)
    total[...] = jnp.zeros_like(total)
    partial[...] = jnp.zeros_like(partial)
    add(blocks, [(tokens, total), (others, partial)])


def second_kernel(add, n, tokens, others, total_before, partial_before, *refs):
    blocks, (total, partial) = refs[:n], refs[n:]
    total[...] = total_before[...]
    partial[...] = partial_before[...]
    add(blocks, [(tokens, total), (others, partial)])


def third_kernel(add, n, tokens, others, total_before, partial_before, *refs):
    blocks, (total, gate, up, sums) = refs[:n], refs[n:]
    total[...] = total_before[...]
    sums[...] = partial_before[...]
    add(blocks, [(tokens, total), (others, sums)])
    wide = gate.shape[1]
    gate[...] = sums[:, :wide]
    up[...] = sums[:, wide:]


def last_kernel(add, n, tokens, total_before, gate_arrived, up_arrived, scale, *refs):
    blocks, (hidden, total) = refs[:n], refs[n:]
    rows, wide = hidden.shape
    theirs = pl.ds(pl.multiple_of((1 - lax.rem(lax.axis_index("fsdp"), 2)) * rows, rows), rows)
    total[:, :wide] = total_before[:, :wide] + gate_arrived[theirs, :]
    total[:, wide:] = total_before[:, wide:] + up_arrived[theirs, :]
    add(blocks, [(tokens, total)])
    gate = total[:, :wide] * scale[...]
    up = total[:, wide:] * scale[...]
    hidden[...] = (gate / (1.0 + jnp.exp(-gate)) * up).astype(hidden.dtype)


def cut_kernel(depth, block, out, sem):
    start = pl.multiple_of(lax.rem(lax.axis_index("fsdp"), 2) * depth, depth)
    copy = pltpu.make_async_copy(block.at[pl.ds(start, depth)], out, sem)
    copy.start()
    copy.wait()


def cut(block):
    depth, wide = block.shape[0] // 2, block.shape[1]
    anywhere = pl.BlockSpec(memory_space=pl.ANY)
    return pl.pallas_call(
        functools.partial(cut_kernel, depth),
        out_shape=jax.ShapeDtypeStruct((depth, wide), block.dtype),
        in_specs=[anywhere],
        out_specs=anywhere,
        scratch_shapes=[pltpu.SemaphoreType.DMA],
        compiler_params=pltpu.CompilerParams(vmem_limit_bytes=vmem_bytes // 16),
        cost_estimate=pl.CostEstimate(flops=0, bytes_accessed=4 * depth * wide, transcendentals=0),
    )(block)


def call(kernel, *, high, specs, arrays, blocks, out_shape, scratch=()):
    n = len(blocks)
    depth, wide = sum(b.shape[0] for b in blocks), blocks[0].shape[1]
    rows = arrays[0].shape[0]
    vmem = pl.BlockSpec(memory_space=pltpu.VMEM)
    return pl.pallas_call(
        functools.partial(kernel, functools.partial(add_blocks, specs, high), n),
        out_shape=out_shape,
        in_specs=[vmem] * (len(arrays) + n),
        out_specs=jax.tree.map(lambda _: vmem, out_shape),
        scratch_shapes=list(scratch),
        compiler_params=pltpu.CompilerParams(vmem_limit_bytes=vmem_bytes),
        cost_estimate=pl.CostEstimate(
            flops=4 * rows * depth * wide, bytes_accessed=2 * depth * wide + 16 * rows * wide, transcendentals=0
        ),
    )(*arrays, *blocks)


def make_on_device(count):
    high = count // 4

    def move(where):
        pairs = []
        for f in range(count):
            y, x, c = where(f // 4, (f // 2) % 2, f % 2)
            pairs.append((f, (y % high) * 4 + (x % 2) * 2 + c % 2))
        return lambda v: lax.ppermute(v, "fsdp", pairs)

    along = move(lambda y, x, c: (y + 1 - 2 * c, x, c))
    across = move(lambda y, x, c: (y, x + 1, c))
    swap = move(lambda y, x, c: (y, x, c + 1))
    core_pairs = [[f, f + 1] for f in range(0, count, 2)]

    def join(v):
        return lax.all_gather(v, "fsdp", axis=0, tiled=True, axis_index_groups=core_pairs)

    def on_device(tokens, norm_gain, gate_weight, up_weight):
        gain = norm_gain[:, None]
        own = jnp.concatenate([gate_weight * gain, up_weight * gain], axis=1).astype(jnp.bfloat16)
        wide = own.shape[1]
        b0 = across(own)
        chip, late = join(own), tokens
        rows = tokens.shape[0]
        sums = jax.ShapeDtypeStruct((rows, wide), jnp.float32)
        step = functools.partial(call, high=high)

        a1 = along(chip)
        b1 = along(join(b0))
        others = swap(late)
        a2 = along(a1)
        b2 = along(b1)
        a3 = along(a2)
        total, partial, scale = step(
            first_kernel,
            specs=[(0, 0, 1), (1, 0, 0), (1, 1, 0), (2, 0, 0)],
            arrays=[tokens, others],
            blocks=[own, a1, b1, a2],
            out_shape=(sums, sums, jax.ShapeDtypeStruct((rows, 1), jnp.float32)),
        )
        b2, total = lax.optimization_barrier((b2, total))
        b3 = along(b2)
        a4 = along(cut(a3))
        total, partial = step(
            second_kernel,
            specs=[(0, 1, 1), (2, 1, 0), (3, 0, 0)],
            arrays=[tokens, others, total, partial],
            blocks=[b0, b2, a3],
            out_shape=(sums, sums),
        )
        b3, total = lax.optimization_barrier((b3, total))
        b4 = along(cut(b3))
        narrow = jax.ShapeDtypeStruct((rows, wide // 2), jnp.float32)
        total, *partial = step(
            third_kernel,
            specs=[(3, 1, 0), (4, 0, 1)],
            arrays=[tokens, others, total, partial],
            blocks=[b3, a4],
            out_shape=(sums, narrow, narrow),
            scratch=[pltpu.VMEM((rows, wide), jnp.float32)],
        )
        partial = [join(v) for v in partial]
        return step(
            last_kernel,
            specs=[(4, 1, 0)],
            arrays=[tokens, total, *partial, scale],
            blocks=[join(b4)],
            out_shape=jax.ShapeDtypeStruct((rows, wide // 2), jnp.bfloat16),
            scratch=[pltpu.VMEM((rows, wide), jnp.float32)],
        )

    return on_device


def solution(mesh):
    return jax.shard_map(
        make_on_device(mesh.shape["fsdp"]),
        mesh=mesh,
        in_specs=(P("fsdp", None), P("fsdp"), P("fsdp", "tensor"), P("fsdp", "tensor")),
        out_specs=P("fsdp", "tensor"),
        check_vma=False,
    )
```

```python
import functools

import jax
import jax.numpy as jnp
from jax import lax
from jax.experimental import pallas as pl
from jax.experimental.pallas import tpu as pltpu
from jax.sharding import PartitionSpec as P

epsilon = 1e-05
vmem_bytes = 16 * 1024 * 1024


def column(spec, high):
    steps, other, half = spec
    index = lax.axis_index("fsdp")
    core = lax.rem(index, 2)
    x = lax.rem(lax.div(index, 2), 2)
    y = lax.rem(lax.div(index, 4) + (steps * (2 * core - 1) + high), high)
    return (y * 2 + (1 - x if other else x)) * 2 + (0, core, 1 - core)[half]


def add_blocks(specs, high, blocks, pairs):
    for spec, block in zip(specs, blocks):
        depth = block.shape[0]
        unit = depth if spec[2] else depth // 2
        start = pl.multiple_of(column(spec, high) * unit, unit)
        for tokens, total in pairs:
            total[...] += jnp.dot(tokens[:, pl.ds(start, depth)], block[...], preferred_element_type=jnp.float32)


def first_kernel(add, n, tokens, others, *refs):
    blocks, (total, partial, scale) = refs[:n], refs[n:]
    values = tokens[...].astype(jnp.float32)
    scale[...] = lax.rsqrt(jnp.mean(values * values, axis=1, keepdims=True) + epsilon)
    total[...] = jnp.zeros_like(total)
    partial[...] = jnp.zeros_like(partial)
    add(blocks, [(tokens, total), (others, partial)])


def second_kernel(add, n, tokens, others, total_before, partial_before, *refs):
    blocks, (total, partial) = refs[:n], refs[n:]
    total[...] = total_before[...]
    partial[...] = partial_before[...]
    add(blocks, [(tokens, total), (others, partial)])


def third_kernel(add, n, tokens, others, total_before, partial_before, *refs):
    blocks, (total, gate, up, sums) = refs[:n], refs[n:]
    total[...] = total_before[...]
    sums[...] = partial_before[...]
    add(blocks, [(tokens, total), (others, sums)])
    wide = gate.shape[1]
    gate[...] = sums[:, :wide]
    up[...] = sums[:, wide:]


def last_kernel(add, n, tokens, total_before, gate_arrived, up_arrived, scale, *refs):
    blocks, (hidden, total) = refs[:n], refs[n:]
    rows, wide = hidden.shape
    theirs = pl.ds(pl.multiple_of((1 - lax.rem(lax.axis_index("fsdp"), 2)) * rows, rows), rows)
    total[:, :wide] = total_before[:, :wide] + gate_arrived[theirs, :]
    total[:, wide:] = total_before[:, wide:] + up_arrived[theirs, :]
    add(blocks, [(tokens, total)])
    gate = total[:, :wide] * scale[...]
    up = total[:, wide:] * scale[...]
    hidden[...] = (gate / (1.0 + jnp.exp(-gate)) * up).astype(hidden.dtype)


def cut_kernel(flip, depth, block, out, sem):
    start = pl.multiple_of(lax.rem(lax.axis_index("fsdp") + flip, 2) * depth, depth)
    copy = pltpu.make_async_copy(block.at[pl.ds(start, depth)], out, sem)
    copy.start()
    copy.wait()


def cut(block, flip=0):
    depth, wide = block.shape[0] // 2, block.shape[1]
    anywhere = pl.BlockSpec(memory_space=pl.ANY)
    return pl.pallas_call(
        functools.partial(cut_kernel, flip, depth),
        out_shape=jax.ShapeDtypeStruct((depth, wide), block.dtype),
        in_specs=[anywhere],
        out_specs=anywhere,
        scratch_shapes=[pltpu.SemaphoreType.DMA],
        compiler_params=pltpu.CompilerParams(vmem_limit_bytes=vmem_bytes // 16),
        cost_estimate=pl.CostEstimate(flops=0, bytes_accessed=4 * depth * wide, transcendentals=0),
    )(block)


def call(kernel, *, high, specs, arrays, blocks, out_shape, scratch=()):
    n = len(blocks)
    depth, wide = sum(b.shape[0] for b in blocks), blocks[0].shape[1]
    rows = arrays[0].shape[0]
    vmem = pl.BlockSpec(memory_space=pltpu.VMEM)
    return pl.pallas_call(
        functools.partial(kernel, functools.partial(add_blocks, specs, high), n),
        out_shape=out_shape,
        in_specs=[vmem] * (len(arrays) + n),
        out_specs=jax.tree.map(lambda _: vmem, out_shape),
        scratch_shapes=list(scratch),
        compiler_params=pltpu.CompilerParams(vmem_limit_bytes=vmem_bytes),
        cost_estimate=pl.CostEstimate(
            flops=4 * rows * depth * wide, bytes_accessed=2 * depth * wide + 16 * rows * wide, transcendentals=0
        ),
    )(*arrays, *blocks)


def make_on_device(count):
    high = count // 4

    def move(where):
        pairs = []
        for f in range(count):
            y, x, c = where(f // 4, (f // 2) % 2, f % 2)
            pairs.append((f, (y % high) * 4 + (x % 2) * 2 + c % 2))
        return lambda v: lax.ppermute(v, "fsdp", pairs)

    along = move(lambda y, x, c: (y + 1 - 2 * c, x, c))
    across = move(lambda y, x, c: (y, x + 1, c))
    swap = move(lambda y, x, c: (y, x, c + 1))
    core_pairs = [[f, f + 1] for f in range(0, count, 2)]

    def join(v):
        return lax.all_gather(v, "fsdp", axis=0, tiled=True, axis_index_groups=core_pairs)

    def on_device(tokens, norm_gain, gate_weight, up_weight):
        gain = norm_gain[:, None]
        own = jnp.concatenate([gate_weight * gain, up_weight * gain], axis=1).astype(jnp.bfloat16)
        wide = own.shape[1]
        b0 = across(own)
        chip = join(own)
        rows = tokens.shape[0]
        sums = jax.ShapeDtypeStruct((rows, wide), jnp.float32)
        step = functools.partial(call, high=high)

        a1 = along(chip)
        beside, late = lax.optimization_barrier((join(b0), tokens))
        b1 = along(beside)
        others = swap(late)
        a2 = along(a1)
        b2 = along(b1)
        a3 = along(a2)
        total, partial, scale = step(
            first_kernel,
            specs=[(0, 0, 1), (1, 0, 0), (1, 1, 0), (2, 0, 0)],
            arrays=[tokens, others],
            blocks=[own, a1, b1, a2],
            out_shape=(sums, sums, jax.ShapeDtypeStruct((rows, 1), jnp.float32)),
        )
        b2, total = lax.optimization_barrier((b2, total))
        b3 = along(cut(b2))
        b3_rest = along(cut(b2, 1))
        a4 = along(cut(a3))
        total, partial = step(
            second_kernel,
            specs=[(0, 1, 1), (2, 1, 0), (3, 0, 0)],
            arrays=[tokens, others, total, partial],
            blocks=[b0, b2, a3],
            out_shape=(sums, sums),
        )
        b3, total = lax.optimization_barrier((b3, total))
        b4 = along(b3)
        narrow = jax.ShapeDtypeStruct((rows, wide // 2), jnp.float32)
        total, *partial = step(
            third_kernel,
            specs=[(3, 1, 1), (3, 1, 2), (4, 0, 1)],
            arrays=[tokens, others, total, partial],
            blocks=[b3, b3_rest, a4],
            out_shape=(sums, narrow, narrow),
            scratch=[pltpu.VMEM((rows, wide), jnp.float32)],
        )
        partial = [join(v) for v in partial]
        return step(
            last_kernel,
            specs=[(4, 1, 0)],
            arrays=[tokens, total, *partial, scale],
            blocks=[join(b4)],
            out_shape=jax.ShapeDtypeStruct((rows, wide // 2), jnp.bfloat16),
            scratch=[pltpu.VMEM((rows, wide), jnp.float32)],
        )

    return on_device


def solution(mesh):
    return jax.shard_map(
        make_on_device(mesh.shape["fsdp"]),
        mesh=mesh,
        in_specs=(P("fsdp", None), P("fsdp"), P("fsdp", "tensor"), P("fsdp", "tensor")),
        out_specs=P("fsdp", "tensor"),
        check_vma=False,
    )
```

```python
import functools

import jax
import jax.numpy as jnp
from jax import lax
from jax.experimental import pallas as pl
from jax.experimental.pallas import tpu as pltpu
from jax.sharding import PartitionSpec as P

epsilon = 1e-05
vmem_bytes = 16 * 1024 * 1024


def column(spec, high):
    steps, other, half = spec
    index = lax.axis_index("fsdp")
    core = lax.rem(index, 2)
    x = lax.rem(lax.div(index, 2), 2)
    y = lax.rem(lax.div(index, 4) + (steps * (2 * core - 1) + high), high)
    return (y * 2 + (1 - x if other else x)) * 2 + (0, core, 1 - core)[half]


def add_blocks(specs, high, blocks, pairs):
    for spec, block in zip(specs, blocks):
        depth = block.shape[0]
        unit = depth if spec[2] else depth // 2
        start = pl.multiple_of(column(spec, high) * unit, unit)
        for tokens, total in pairs:
            total[...] += jnp.dot(tokens[:, pl.ds(start, depth)], block[...], preferred_element_type=jnp.float32)


def first_kernel(add, n, tokens, others, *refs):
    blocks, (total, partial, scale) = refs[:n], refs[n:]
    values = tokens[...].astype(jnp.float32)
    scale[...] = lax.rsqrt(jnp.mean(values * values, axis=1, keepdims=True) + epsilon)
    total[...] = jnp.zeros_like(total)
    partial[...] = jnp.zeros_like(partial)
    add(blocks, [(tokens, total), (others, partial)])


def second_kernel(add, n, tokens, others, total_before, partial_before, *refs):
    blocks, (total, gate, up, partial) = refs[:n], refs[n:]
    total[...] = total_before[...]
    partial[...] = partial_before[...]
    add(blocks, [(tokens, total), (others, partial)])
    wide = gate.shape[1]
    gate[...] = partial[:, :wide]
    up[...] = partial[:, wide:]


def third_kernel(add, n, tokens, others, total_before, *refs):
    blocks, (total, leaving, partial) = refs[:n], refs[n:]
    total[...] = total_before[...]
    partial[...] = jnp.zeros_like(partial)
    add(blocks, [(tokens, total), (others, partial)])
    leaving[...] = partial[...].astype(leaving.dtype)


def last_kernel(add, n, total, gate_arrived, up_arrived, late, scale, hidden):
    rows, wide = hidden.shape
    theirs = pl.ds(pl.multiple_of((1 - lax.rem(lax.axis_index("fsdp"), 2)) * rows, rows), rows)
    gate = (total[:, :wide] + gate_arrived[theirs, :] + late[theirs, :wide].astype(jnp.float32)) * scale[...]
    up = (total[:, wide:] + up_arrived[theirs, :] + late[theirs, wide:].astype(jnp.float32)) * scale[...]
    hidden[...] = (gate / (1.0 + jnp.exp(-gate)) * up).astype(hidden.dtype)


def cut_kernel(flip, depth, block, out, sem):
    start = pl.multiple_of(lax.rem(lax.axis_index("fsdp") + flip, 2) * depth, depth)
    copy = pltpu.make_async_copy(block.at[pl.ds(start, depth)], out, sem)
    copy.start()
    copy.wait()


def cut(block, flip=0):
    depth, wide = block.shape[0] // 2, block.shape[1]
    anywhere = pl.BlockSpec(memory_space=pl.ANY)
    return pl.pallas_call(
        functools.partial(cut_kernel, flip, depth),
        out_shape=jax.ShapeDtypeStruct((depth, wide), block.dtype),
        in_specs=[anywhere],
        out_specs=anywhere,
        scratch_shapes=[pltpu.SemaphoreType.DMA],
        compiler_params=pltpu.CompilerParams(vmem_limit_bytes=vmem_bytes // 16),
        cost_estimate=pl.CostEstimate(flops=0, bytes_accessed=4 * depth * wide, transcendentals=0),
    )(block)


def call(kernel, *, high, sum_width, specs, arrays, blocks, out_shape, scratch=()):
    n = len(blocks)
    depth = sum(b.shape[0] for b in blocks)
    rows, wide = arrays[0].shape[0], sum_width
    vmem = pl.BlockSpec(memory_space=pltpu.VMEM)
    return pl.pallas_call(
        functools.partial(kernel, functools.partial(add_blocks, specs, high), n),
        out_shape=out_shape,
        in_specs=[vmem] * (len(arrays) + n),
        out_specs=jax.tree.map(lambda _: vmem, out_shape),
        scratch_shapes=list(scratch),
        compiler_params=pltpu.CompilerParams(vmem_limit_bytes=vmem_bytes),
        cost_estimate=pl.CostEstimate(
            flops=4 * rows * depth * wide, bytes_accessed=2 * depth * wide + 16 * rows * wide, transcendentals=0
        ),
    )(*arrays, *blocks)


def make_on_device(count):
    high = count // 4

    def move(where):
        pairs = []
        for f in range(count):
            y, x, c = where(f // 4, (f // 2) % 2, f % 2)
            pairs.append((f, (y % high) * 4 + (x % 2) * 2 + c % 2))
        return lambda v: lax.ppermute(v, "fsdp", pairs)

    along = move(lambda y, x, c: (y + 1 - 2 * c, x, c))
    across = move(lambda y, x, c: (y, x + 1, c))
    swap = move(lambda y, x, c: (y, x, c + 1))
    core_pairs = [[f, f + 1] for f in range(0, count, 2)]

    def join(v):
        return lax.all_gather(v, "fsdp", axis=0, tiled=True, axis_index_groups=core_pairs)

    def on_device(tokens, norm_gain, gate_weight, up_weight):
        gain = norm_gain[:, None]
        own = jnp.concatenate([gate_weight * gain, up_weight * gain], axis=1).astype(jnp.bfloat16)
        wide = own.shape[1]
        b0 = across(own)
        chip = join(own)
        rows = tokens.shape[0]
        sums = jax.ShapeDtypeStruct((rows, wide), jnp.float32)
        step = functools.partial(call, high=high, sum_width=wide)

        a1 = along(chip)
        beside, late = lax.optimization_barrier((join(b0), tokens))
        b1 = along(beside)
        others = swap(late)
        a2 = along(a1)
        b2 = along(b1)
        a3 = along(a2)
        total, partial, scale = step(
            first_kernel,
            specs=[(0, 0, 1), (1, 0, 0), (1, 1, 0), (2, 0, 0)],
            arrays=[tokens, others],
            blocks=[own, a1, b1, a2],
            out_shape=(sums, sums, jax.ShapeDtypeStruct((rows, 1), jnp.float32)),
        )
        b2, total = lax.optimization_barrier((b2, total))
        b3 = along(cut(b2))
        b3_rest = along(cut(b2, 1))
        a4 = along(cut(a3))
        narrow = jax.ShapeDtypeStruct((rows, wide // 2), jnp.float32)
        total, gate, up = step(
            second_kernel,
            specs=[(0, 1, 1), (2, 1, 0), (3, 0, 0)],
            arrays=[tokens, others, total, partial],
            blocks=[b0, b2, a3],
            out_shape=(sums, narrow, narrow),
            scratch=[pltpu.VMEM((rows, wide), jnp.float32)],
        )
        b3, total = lax.optimization_barrier((b3, total))
        b4 = along(b3)
        total, late = step(
            third_kernel,
            specs=[(3, 1, 1), (3, 1, 2), (4, 0, 1), (4, 1, 1)],
            arrays=[tokens, others, total],
            blocks=[b3, b3_rest, a4, b4],
            out_shape=(sums, jax.ShapeDtypeStruct((rows, wide), jnp.bfloat16)),
            scratch=[pltpu.VMEM((rows, wide), jnp.float32)],
        )
        return step(
            last_kernel,
            specs=[],
            arrays=[total, join(gate), join(up), join(late), scale],
            blocks=[],
            out_shape=jax.ShapeDtypeStruct((rows, wide // 2), jnp.bfloat16),
        )

    return on_device


def solution(mesh):
    return jax.shard_map(
        make_on_device(mesh.shape["fsdp"]),
        mesh=mesh,
        in_specs=(P("fsdp", None), P("fsdp"), P("fsdp", "tensor"), P("fsdp", "tensor")),
        out_specs=P("fsdp", "tensor"),
        check_vma=False,
    )
```

```python
import functools

import jax
import jax.numpy as jnp
from jax import lax
from jax.experimental import pallas as pl
from jax.experimental.pallas import tpu as pltpu
from jax.sharding import PartitionSpec as P

epsilon = 1e-05
vmem_bytes = 16 * 1024 * 1024


def column(spec, high):
    steps, other, half = spec
    index = lax.axis_index("fsdp")
    core = lax.rem(index, 2)
    x = lax.rem(lax.div(index, 2), 2)
    y = lax.rem(lax.div(index, 4) + (steps * (2 * core - 1) + high), high)
    return (y * 2 + (1 - x if other else x)) * 2 + (0, core, 1 - core)[half]


def theirs(ref):
    rows = ref.shape[0]
    return pl.ds(pl.multiple_of((1 - lax.rem(lax.axis_index("fsdp"), 2)) * rows, rows), rows)


def add_blocks(specs, high, blocks, pairs):
    for spec, block in zip(specs, blocks):
        depth = block.shape[0]
        unit = depth if spec[2] else depth // 2
        start = pl.multiple_of(column(spec, high) * unit, unit)
        for tokens, total in pairs:
            left = tokens[theirs(total) if tokens.shape[0] > total.shape[0] else slice(None), pl.ds(start, depth)]
            total[...] += jnp.dot(left, block[...], preferred_element_type=jnp.float32)


def first_kernel(add, n, tokens, others, *refs):
    blocks, (total, partial, scale) = refs[:n], refs[n:]
    values = tokens[...].astype(jnp.float32)
    scale[...] = lax.rsqrt(jnp.mean(values * values, axis=1, keepdims=True) + epsilon)
    total[...] = jnp.zeros_like(total)
    partial[...] = jnp.zeros_like(partial)
    add(blocks, [(tokens, total), (others, partial)])


def second_kernel(add, n, tokens, others, total_before, partial_before, *refs):
    blocks, (total, gate, up, partial) = refs[:n], refs[n:]
    total[...] = total_before[...]
    partial[...] = partial_before[...]
    add(blocks, [(tokens, total), (others, partial)])
    wide = gate.shape[1]
    gate[...] = partial[:, :wide]
    up[...] = partial[:, wide:]


def third_kernel(add, n, tokens, others, total_before, *refs):
    blocks, (total, leaving, partial) = refs[:n], refs[n:]
    total[...] = total_before[...]
    partial[...] = jnp.zeros_like(partial)
    add(blocks, [(tokens, total), (others, partial)])
    leaving[...] = partial[...].astype(leaving.dtype)


def last_kernel(add, n, total, gate_arrived, up_arrived, late, scale, hidden):
    wide = hidden.shape[1]
    other = theirs(hidden)
    gate = (total[:, :wide] + gate_arrived[other, :] + late[other, :wide].astype(jnp.float32)) * scale[...]
    up = (total[:, wide:] + up_arrived[other, :] + late[other, wide:].astype(jnp.float32)) * scale[...]
    hidden[...] = (gate / (1.0 + jnp.exp(-gate)) * up).astype(hidden.dtype)


def cut_kernel(flip, depth, block, out, sem):
    start = pl.multiple_of(lax.rem(lax.axis_index("fsdp") + flip, 2) * depth, depth)
    copy = pltpu.make_async_copy(block.at[pl.ds(start, depth)], out, sem)
    copy.start()
    copy.wait()


def cut(block, flip=0):
    depth, wide = block.shape[0] // 2, block.shape[1]
    anywhere = pl.BlockSpec(memory_space=pl.ANY)
    return pl.pallas_call(
        functools.partial(cut_kernel, flip, depth),
        out_shape=jax.ShapeDtypeStruct((depth, wide), block.dtype),
        in_specs=[anywhere],
        out_specs=anywhere,
        scratch_shapes=[pltpu.SemaphoreType.DMA],
        compiler_params=pltpu.CompilerParams(vmem_limit_bytes=vmem_bytes // 16),
        cost_estimate=pl.CostEstimate(flops=0, bytes_accessed=4 * depth * wide, transcendentals=0),
    )(block)


def call(kernel, *, high, sum_width, specs, arrays, blocks, out_shape, scratch=()):
    n = len(blocks)
    depth = sum(b.shape[0] for b in blocks)
    rows, wide = arrays[0].shape[0], sum_width
    vmem = pl.BlockSpec(memory_space=pltpu.VMEM)
    return pl.pallas_call(
        functools.partial(kernel, functools.partial(add_blocks, specs, high), n),
        out_shape=out_shape,
        in_specs=[vmem] * (len(arrays) + n),
        out_specs=jax.tree.map(lambda _: vmem, out_shape),
        scratch_shapes=list(scratch),
        compiler_params=pltpu.CompilerParams(vmem_limit_bytes=vmem_bytes),
        cost_estimate=pl.CostEstimate(
            flops=4 * rows * depth * wide, bytes_accessed=2 * depth * wide + 16 * rows * wide, transcendentals=0
        ),
    )(*arrays, *blocks)


def make_on_device(count):
    high = count // 4

    def move(where):
        pairs = []
        for f in range(count):
            y, x, c = where(f // 4, (f // 2) % 2, f % 2)
            pairs.append((f, (y % high) * 4 + (x % 2) * 2 + c % 2))
        return lambda v: lax.ppermute(v, "fsdp", pairs)

    along = move(lambda y, x, c: (y + 1 - 2 * c, x, c))
    across = move(lambda y, x, c: (y, x + 1, c))
    core_pairs = [[f, f + 1] for f in range(0, count, 2)]

    def join(v):
        return lax.all_gather(v, "fsdp", axis=0, tiled=True, axis_index_groups=core_pairs)

    def on_device(tokens, norm_gain, gate_weight, up_weight):
        gain = norm_gain[:, None]
        own = jnp.concatenate([gate_weight * gain, up_weight * gain], axis=1).astype(jnp.bfloat16)
        wide = own.shape[1]
        b0 = across(own)
        chip = join(own)
        rows = tokens.shape[0]
        sums = jax.ShapeDtypeStruct((rows, wide), jnp.float32)
        step = functools.partial(call, high=high, sum_width=wide)

        a1 = along(chip)
        b1 = along(join(b0))
        others = join(tokens)
        a2 = along(a1)
        b2 = along(b1)
        a3 = along(a2)
        total, partial, scale = step(
            first_kernel,
            specs=[(0, 0, 1), (1, 0, 0), (1, 1, 0), (2, 0, 0)],
            arrays=[tokens, others],
            blocks=[own, a1, b1, a2],
            out_shape=(sums, sums, jax.ShapeDtypeStruct((rows, 1), jnp.float32)),
        )
        b2, total = lax.optimization_barrier((b2, total))
        b3 = along(cut(b2))
        b3_rest = along(cut(b2, 1))
        a4 = along(cut(a3))
        narrow = jax.ShapeDtypeStruct((rows, wide // 2), jnp.float32)
        total, gate, up = step(
            second_kernel,
            specs=[(0, 1, 1), (2, 1, 0), (3, 0, 0)],
            arrays=[tokens, others, total, partial],
            blocks=[b0, b2, a3],
            out_shape=(sums, narrow, narrow),
            scratch=[pltpu.VMEM((rows, wide), jnp.float32)],
        )
        b3, total = lax.optimization_barrier((b3, total))
        b4 = along(b3)
        total, late = step(
            third_kernel,
            specs=[(3, 1, 1), (3, 1, 2), (4, 0, 1), (4, 1, 1)],
            arrays=[tokens, others, total],
            blocks=[b3, b3_rest, a4, b4],
            out_shape=(sums, jax.ShapeDtypeStruct((rows, wide), jnp.bfloat16)),
            scratch=[pltpu.VMEM((rows, wide), jnp.float32)],
        )
        return step(
            last_kernel,
            specs=[],
            arrays=[total, join(gate), join(up), join(late), scale],
            blocks=[],
            out_shape=jax.ShapeDtypeStruct((rows, wide // 2), jnp.bfloat16),
        )

    return on_device


def solution(mesh):
    return jax.shard_map(
        make_on_device(mesh.shape["fsdp"]),
        mesh=mesh,
        in_specs=(P("fsdp", None), P("fsdp"), P("fsdp", "tensor"), P("fsdp", "tensor")),
        out_specs=P("fsdp", "tensor"),
        check_vma=False,
    )
```

```python
import functools

import jax
import jax.numpy as jnp
from jax import lax
from jax.experimental import pallas as pl
from jax.experimental.pallas import tpu as pltpu
from jax.sharding import PartitionSpec as P

epsilon = 1e-05
vmem_bytes = 16 * 1024 * 1024


def column(spec, high):
    steps, other, half = spec
    index = lax.axis_index("fsdp")
    core = lax.rem(index, 2)
    x = lax.rem(lax.div(index, 2), 2)
    y = lax.rem(lax.div(index, 4) + (steps * (2 * core - 1) + high), high)
    return (y * 2 + (1 - x if other else x)) * 2 + (0, core, 1 - core)[half]


def add_blocks(specs, high, blocks, pairs):
    for spec, block in zip(specs, blocks):
        depth = block.shape[0]
        unit = depth if spec[2] else depth // 2
        start = pl.multiple_of(column(spec, high) * unit, unit)
        for tokens, total in pairs:
            total[...] += jnp.dot(tokens[:, pl.ds(start, depth)], block[...], preferred_element_type=jnp.float32)


def first_kernel(add, n, tokens, others, *refs):
    blocks, (total, partial, scale) = refs[:n], refs[n:]
    values = tokens[...].astype(jnp.float32)
    scale[...] = lax.rsqrt(jnp.mean(values * values, axis=1, keepdims=True) + epsilon)
    total[...] = jnp.zeros_like(total)
    partial[...] = jnp.zeros_like(partial)
    add(blocks, [(tokens, total), (others, partial)])


def second_kernel(add, n, tokens, others, total_before, partial_before, *refs):
    blocks, (total, gate, up, partial) = refs[:n], refs[n:]
    total[...] = total_before[...]
    partial[...] = partial_before[...]
    add(blocks, [(tokens, total), (others, partial)])
    wide = gate.shape[1]
    gate[...] = partial[:, :wide]
    up[...] = partial[:, wide:]


def their_rows(rows):
    return pl.ds(pl.multiple_of((1 - lax.rem(lax.axis_index("fsdp"), 2)) * rows, rows), rows)


def third_kernel(add, n, tokens, others, total_before, gate_arrived, up_arrived, *refs):
    blocks, (total, partial) = refs[:n], refs[n:]
    wide = gate_arrived.shape[1]
    theirs = their_rows(total.shape[0])
    total[:, :wide] = total_before[:, :wide] + gate_arrived[theirs, :]
    total[:, wide:] = total_before[:, wide:] + up_arrived[theirs, :]
    partial[...] = jnp.zeros_like(partial)
    add(blocks, [(tokens, total), (others, partial)])


def fourth_kernel(add, n, tokens, others, total_before, partial_before, *refs):
    blocks, (total, leaving, partial) = refs[:n], refs[n:]
    total[...] = total_before[...]
    partial[...] = partial_before[...]
    add(blocks, [(tokens, total), (others, partial)])
    leaving[...] = partial[...].astype(leaving.dtype)


def last_kernel(add, n, total, late, scale, hidden):
    rows, wide = hidden.shape
    theirs = their_rows(rows)
    gate = (total[:, :wide] + late[theirs, :wide].astype(jnp.float32)) * scale[...]
    up = (total[:, wide:] + late[theirs, wide:].astype(jnp.float32)) * scale[...]
    hidden[...] = (gate / (1.0 + jnp.exp(-gate)) * up).astype(hidden.dtype)


def cut_kernel(flip, depth, block, out, sem):
    start = pl.multiple_of(lax.rem(lax.axis_index("fsdp") + flip, 2) * depth, depth)
    copy = pltpu.make_async_copy(block.at[pl.ds(start, depth)], out, sem)
    copy.start()
    copy.wait()


def cut(block, flip=0):
    depth, wide = block.shape[0] // 2, block.shape[1]
    anywhere = pl.BlockSpec(memory_space=pl.ANY)
    return pl.pallas_call(
        functools.partial(cut_kernel, flip, depth),
        out_shape=jax.ShapeDtypeStruct((depth, wide), block.dtype),
        in_specs=[anywhere],
        out_specs=anywhere,
        scratch_shapes=[pltpu.SemaphoreType.DMA],
        compiler_params=pltpu.CompilerParams(vmem_limit_bytes=vmem_bytes // 16),
        cost_estimate=pl.CostEstimate(flops=0, bytes_accessed=4 * depth * wide, transcendentals=0),
    )(block)


def call(kernel, *, high, sum_width, specs, arrays, blocks, out_shape, scratch=()):
    n = len(blocks)
    depth = sum(b.shape[0] for b in blocks)
    rows, wide = arrays[0].shape[0], sum_width
    vmem = pl.BlockSpec(memory_space=pltpu.VMEM)
    return pl.pallas_call(
        functools.partial(kernel, functools.partial(add_blocks, specs, high), n),
        out_shape=out_shape,
        in_specs=[vmem] * (len(arrays) + n),
        out_specs=jax.tree.map(lambda _: vmem, out_shape),
        scratch_shapes=list(scratch),
        compiler_params=pltpu.CompilerParams(vmem_limit_bytes=vmem_bytes),
        cost_estimate=pl.CostEstimate(
            flops=4 * rows * depth * wide, bytes_accessed=2 * depth * wide + 16 * rows * wide, transcendentals=0
        ),
    )(*arrays, *blocks)


def make_on_device(count):
    high = count // 4

    def move(where):
        pairs = []
        for f in range(count):
            y, x, c = where(f // 4, (f // 2) % 2, f % 2)
            pairs.append((f, (y % high) * 4 + (x % 2) * 2 + c % 2))
        return lambda v: lax.ppermute(v, "fsdp", pairs)

    along = move(lambda y, x, c: (y + 1 - 2 * c, x, c))
    across = move(lambda y, x, c: (y, x + 1, c))
    swap = move(lambda y, x, c: (y, x, c + 1))
    core_pairs = [[f, f + 1] for f in range(0, count, 2)]

    def join(v):
        return lax.all_gather(v, "fsdp", axis=0, tiled=True, axis_index_groups=core_pairs)

    def on_device(tokens, norm_gain, gate_weight, up_weight):
        gain = norm_gain[:, None]
        own = jnp.concatenate([gate_weight * gain, up_weight * gain], axis=1).astype(jnp.bfloat16)
        wide = own.shape[1]
        b0 = across(own)
        chip, late = lax.optimization_barrier((join(own), tokens))
        rows = tokens.shape[0]
        sums = jax.ShapeDtypeStruct((rows, wide), jnp.float32)
        step = functools.partial(call, high=high, sum_width=wide)

        a1 = along(chip)
        b1 = along(join(b0))
        others = swap(late)
        a2 = along(a1)
        b2 = along(b1)
        a3 = along(a2)
        total, partial, scale = step(
            first_kernel,
            specs=[(0, 0, 1), (1, 0, 0), (1, 1, 0), (2, 0, 0)],
            arrays=[tokens, others],
            blocks=[own, a1, b1, a2],
            out_shape=(sums, sums, jax.ShapeDtypeStruct((rows, 1), jnp.float32)),
        )
        b2, total = lax.optimization_barrier((b2, total))
        b3 = along(cut(b2))
        b3_rest = along(cut(b2, 1))
        a4 = along(cut(a3))
        narrow = jax.ShapeDtypeStruct((rows, wide // 2), jnp.float32)
        total, gate, up = step(
            second_kernel,
            specs=[(0, 1, 1), (2, 1, 0), (3, 0, 0)],
            arrays=[tokens, others, total, partial],
            blocks=[b0, b2, a3],
            out_shape=(sums, narrow, narrow),
            scratch=[pltpu.VMEM((rows, wide), jnp.float32)],
        )
        b3, total = lax.optimization_barrier((b3, total))
        b4 = along(b3)
        total, partial = step(
            third_kernel,
            specs=[(3, 1, 1), (3, 1, 2), (4, 0, 1)],
            arrays=[tokens, others, total, join(gate), join(up)],
            blocks=[b3, b3_rest, a4],
            out_shape=(sums, sums),
        )
        b4, total = lax.optimization_barrier((b4, total))
        total, late = step(
            fourth_kernel,
            specs=[(4, 1, 1)],
            arrays=[tokens, others, total, partial],
            blocks=[b4],
            out_shape=(sums, jax.ShapeDtypeStruct((rows, wide), jnp.bfloat16)),
            scratch=[pltpu.VMEM((rows, wide), jnp.float32)],
        )
        return step(
            last_kernel,
            specs=[],
            arrays=[total, join(late), scale],
            blocks=[],
            out_shape=jax.ShapeDtypeStruct((rows, wide // 2), jnp.bfloat16),
        )

    return on_device


def solution(mesh):
    return jax.shard_map(
        make_on_device(mesh.shape["fsdp"]),
        mesh=mesh,
        in_specs=(P("fsdp", None), P("fsdp"), P("fsdp", "tensor"), P("fsdp", "tensor")),
        out_specs=P("fsdp", "tensor"),
        check_vma=False,
    )
```

```python
import functools

import jax
import jax.numpy as jnp
from jax import lax
from jax.experimental import pallas as pl
from jax.experimental.pallas import tpu as pltpu
from jax.sharding import PartitionSpec as P

epsilon = 1e-05
vmem_bytes = 16 * 1024 * 1024


def column(spec, high):
    steps, other, half = spec
    index = lax.axis_index("fsdp")
    core = lax.rem(index, 2)
    x = lax.rem(lax.div(index, 2), 2)
    y = lax.rem(lax.div(index, 4) + (steps * (2 * core - 1) + high), high)
    return (y * 2 + (1 - x if other else x)) * 2 + (0, core, 1 - core)[half]


def add_blocks(specs, high, blocks, pairs):
    for spec, block in zip(specs, blocks):
        depth = block.shape[0]
        unit = depth if spec[2] else depth // 2
        start = pl.multiple_of(column(spec, high) * unit, unit)
        for tokens, total in pairs:
            total[...] += jnp.dot(tokens[:, pl.ds(start, depth)], block[...], preferred_element_type=jnp.float32)


def first_kernel(add, n, tokens, others, *refs):
    blocks, (total, partial, scale) = refs[:n], refs[n:]
    values = tokens[...].astype(jnp.float32)
    scale[...] = lax.rsqrt(jnp.mean(values * values, axis=1, keepdims=True) + epsilon)
    total[...] = jnp.zeros_like(total)
    partial[...] = jnp.zeros_like(partial)
    add(blocks, [(tokens, total), (others, partial)])


def second_kernel(add, n, tokens, others, total_before, partial_before, *refs):
    blocks, (total, gate, up, partial) = refs[:n], refs[n:]
    total[...] = total_before[...]
    partial[...] = partial_before[...]
    add(blocks, [(tokens, total), (others, partial)])
    wide = gate.shape[1]
    gate[...] = partial[:, :wide]
    up[...] = partial[:, wide:]


def their_rows(rows):
    return pl.ds(pl.multiple_of((1 - lax.rem(lax.axis_index("fsdp"), 2)) * rows, rows), rows)


def third_kernel(add, n, tokens, others, total_before, gate_arrived, up_arrived, *refs):
    blocks, (total, partial) = refs[:n], refs[n:]
    wide = gate_arrived.shape[1]
    theirs = their_rows(total.shape[0])
    total[:, :wide] = total_before[:, :wide] + gate_arrived[theirs, :]
    total[:, wide:] = total_before[:, wide:] + up_arrived[theirs, :]
    partial[...] = jnp.zeros_like(partial)
    add(blocks, [(tokens, total), (others, partial)])


def fourth_kernel(add, n, tokens, others, total_before, partial_before, *refs):
    blocks, (total, leaving, partial) = refs[:n], refs[n:]
    total[...] = total_before[...]
    partial[...] = partial_before[...]
    add(blocks, [(tokens, total), (others, partial)])
    leaving[...] = partial[...].astype(leaving.dtype)


def last_kernel(add, n, total, late, scale, hidden):
    rows, wide = hidden.shape
    theirs = their_rows(rows)
    gate = (total[:, :wide] + late[theirs, :wide].astype(jnp.float32)) * scale[...]
    up = (total[:, wide:] + late[theirs, wide:].astype(jnp.float32)) * scale[...]
    hidden[...] = (gate / (1.0 + jnp.exp(-gate)) * up).astype(hidden.dtype)


def cut_kernel(flip, depth, block, out, sem):
    start = pl.multiple_of(lax.rem(lax.axis_index("fsdp") + flip, 2) * depth, depth)
    copy = pltpu.make_async_copy(block.at[pl.ds(start, depth)], out, sem)
    copy.start()
    copy.wait()


def cut(block, flip=0):
    depth, wide = block.shape[0] // 2, block.shape[1]
    anywhere = pl.BlockSpec(memory_space=pl.ANY)
    return pl.pallas_call(
        functools.partial(cut_kernel, flip, depth),
        out_shape=jax.ShapeDtypeStruct((depth, wide), block.dtype),
        in_specs=[anywhere],
        out_specs=anywhere,
        scratch_shapes=[pltpu.SemaphoreType.DMA],
        compiler_params=pltpu.CompilerParams(vmem_limit_bytes=vmem_bytes // 16),
        cost_estimate=pl.CostEstimate(flops=0, bytes_accessed=4 * depth * wide, transcendentals=0),
    )(block)


def call(kernel, *, high, sum_width, specs, arrays, blocks, out_shape, scratch=()):
    n = len(blocks)
    depth = sum(b.shape[0] for b in blocks)
    rows, wide = arrays[0].shape[0], sum_width
    vmem = pl.BlockSpec(memory_space=pltpu.VMEM)
    return pl.pallas_call(
        functools.partial(kernel, functools.partial(add_blocks, specs, high), n),
        out_shape=out_shape,
        in_specs=[vmem] * (len(arrays) + n),
        out_specs=jax.tree.map(lambda _: vmem, out_shape),
        scratch_shapes=list(scratch),
        compiler_params=pltpu.CompilerParams(vmem_limit_bytes=vmem_bytes),
        cost_estimate=pl.CostEstimate(
            flops=4 * rows * depth * wide, bytes_accessed=2 * depth * wide + 16 * rows * wide, transcendentals=0
        ),
    )(*arrays, *blocks)


def make_on_device(count):
    high = count // 4

    def move(where):
        pairs = []
        for f in range(count):
            y, x, c = where(f // 4, (f // 2) % 2, f % 2)
            pairs.append((f, (y % high) * 4 + (x % 2) * 2 + c % 2))
        return lambda v: lax.ppermute(v, "fsdp", pairs)

    along = move(lambda y, x, c: (y + 1 - 2 * c, x, c))
    across = move(lambda y, x, c: (y, x + 1, c))
    swap = move(lambda y, x, c: (y, x, c + 1))
    core_pairs = [[f, f + 1] for f in range(0, count, 2)]

    def join(v):
        return lax.all_gather(v, "fsdp", axis=0, tiled=True, axis_index_groups=core_pairs)

    def on_device(tokens, norm_gain, gate_weight, up_weight):
        gain = norm_gain[:, None]
        own = jnp.concatenate([gate_weight * gain, up_weight * gain], axis=1).astype(jnp.bfloat16)
        wide = own.shape[1]
        b0 = across(own)
        chip, late = lax.optimization_barrier((join(own), tokens))
        rows = tokens.shape[0]
        sums = jax.ShapeDtypeStruct((rows, wide), jnp.float32)
        step = functools.partial(call, high=high, sum_width=wide)

        a1 = along(chip)
        b1 = along(join(b0))
        others = swap(late)
        a2 = along(a1)
        b2 = along(b1)
        a3 = along(cut(a2))
        a3_rest = along(cut(a2, 1))
        total, partial, scale = step(
            first_kernel,
            specs=[(0, 0, 1), (1, 0, 0), (1, 1, 0), (2, 0, 0)],
            arrays=[tokens, others],
            blocks=[own, a1, b1, a2],
            out_shape=(sums, sums, jax.ShapeDtypeStruct((rows, 1), jnp.float32)),
        )
        b2, total = lax.optimization_barrier((b2, total))
        b3 = along(cut(b2))
        b3_rest = along(cut(b2, 1))
        a4 = along(a3)
        narrow = jax.ShapeDtypeStruct((rows, wide // 2), jnp.float32)
        total, gate, up = step(
            second_kernel,
            specs=[(0, 1, 1), (2, 1, 0), (3, 0, 1), (3, 0, 2)],
            arrays=[tokens, others, total, partial],
            blocks=[b0, b2, a3, a3_rest],
            out_shape=(sums, narrow, narrow),
            scratch=[pltpu.VMEM((rows, wide), jnp.float32)],
        )
        b3, total = lax.optimization_barrier((b3, total))
        b4 = along(b3)
        total, partial = step(
            third_kernel,
            specs=[(3, 1, 1), (3, 1, 2), (4, 0, 1)],
            arrays=[tokens, others, total, join(gate), join(up)],
            blocks=[b3, b3_rest, a4],
            out_shape=(sums, sums),
        )
        b4, total = lax.optimization_barrier((b4, total))
        total, late = step(
            fourth_kernel,
            specs=[(4, 1, 1)],
            arrays=[tokens, others, total, partial],
            blocks=[b4],
            out_shape=(sums, jax.ShapeDtypeStruct((rows, wide), jnp.bfloat16)),
            scratch=[pltpu.VMEM((rows, wide), jnp.float32)],
        )
        return step(
            last_kernel,
            specs=[],
            arrays=[total, join(late), scale],
            blocks=[],
            out_shape=jax.ShapeDtypeStruct((rows, wide // 2), jnp.bfloat16),
        )

    return on_device


def solution(mesh):
    return jax.shard_map(
        make_on_device(mesh.shape["fsdp"]),
        mesh=mesh,
        in_specs=(P("fsdp", None), P("fsdp"), P("fsdp", "tensor"), P("fsdp", "tensor")),
        out_specs=P("fsdp", "tensor"),
        check_vma=False,
    )
```

```python
import functools

import jax
import jax.numpy as jnp
from jax import lax
from jax.experimental import pallas as pl
from jax.experimental.pallas import tpu as pltpu
from jax.sharding import PartitionSpec as P

epsilon = 1e-05
vmem_bytes = 16 * 1024 * 1024


def column(spec, high):
    steps, other, half = spec
    index = lax.axis_index("fsdp")
    core = lax.rem(index, 2)
    x = lax.rem(lax.div(index, 2), 2)
    y = lax.rem(lax.div(index, 4) + (steps * (2 * core - 1) + high), high)
    return (y * 2 + (1 - x if other else x)) * 2 + (0, core, 1 - core)[half]


def add_blocks(specs, high, blocks, pairs):
    for spec, block in zip(specs, blocks):
        depth = block.shape[0]
        unit = depth if spec[2] else depth // 2
        start = pl.multiple_of(column(spec, high) * unit, unit)
        for tokens, total in pairs:
            total[...] += jnp.dot(tokens[:, pl.ds(start, depth)], block[...], preferred_element_type=jnp.float32)


def first_kernel(add, n, tokens, others, *refs):
    blocks, (total, partial, scale) = refs[:n], refs[n:]
    values = tokens[...].astype(jnp.float32)
    scale[...] = lax.rsqrt(jnp.mean(values * values, axis=1, keepdims=True) + epsilon)
    total[...] = jnp.zeros_like(total)
    partial[...] = jnp.zeros_like(partial)
    add(blocks, [(tokens, total), (others, partial)])


def second_kernel(add, n, tokens, others, total_before, partial_before, *refs):
    blocks, (total, gate, up, partial) = refs[:n], refs[n:]
    total[...] = total_before[...]
    partial[...] = partial_before[...]
    add(blocks, [(tokens, total), (others, partial)])
    wide = gate.shape[1]
    gate[...] = partial[:, :wide]
    up[...] = partial[:, wide:]


def their_rows(rows):
    return pl.ds(pl.multiple_of((1 - lax.rem(lax.axis_index("fsdp"), 2)) * rows, rows), rows)


def third_kernel(add, n, tokens, others, total_before, gate_arrived, up_arrived, *refs):
    blocks, (total, leaving, partial) = refs[:n], refs[n:]
    wide = gate_arrived.shape[1]
    theirs = their_rows(total.shape[0])
    total[:, :wide] = total_before[:, :wide] + gate_arrived[theirs, :]
    total[:, wide:] = total_before[:, wide:] + up_arrived[theirs, :]
    partial[...] = jnp.zeros_like(partial)
    add(blocks, [(tokens, total), (others, partial)])
    leaving[...] = partial[...].astype(leaving.dtype)


def last_kernel(add, n, tokens, total_before, late, scale, *refs):
    blocks, (hidden, total) = refs[:n], refs[n:]
    rows, wide = hidden.shape
    total[...] = total_before[...] + late[their_rows(rows), :].astype(jnp.float32)
    add(blocks, [(tokens, total)])
    gate = total[:, :wide] * scale[...]
    up = total[:, wide:] * scale[...]
    hidden[...] = (gate / (1.0 + jnp.exp(-gate)) * up).astype(hidden.dtype)


def cut_kernel(flip, depth, block, out, sem):
    start = pl.multiple_of(lax.rem(lax.axis_index("fsdp") + flip, 2) * depth, depth)
    copy = pltpu.make_async_copy(block.at[pl.ds(start, depth)], out, sem)
    copy.start()
    copy.wait()


def cut(block, flip=0):
    depth, wide = block.shape[0] // 2, block.shape[1]
    anywhere = pl.BlockSpec(memory_space=pl.ANY)
    return pl.pallas_call(
        functools.partial(cut_kernel, flip, depth),
        out_shape=jax.ShapeDtypeStruct((depth, wide), block.dtype),
        in_specs=[anywhere],
        out_specs=anywhere,
        scratch_shapes=[pltpu.SemaphoreType.DMA],
        compiler_params=pltpu.CompilerParams(vmem_limit_bytes=vmem_bytes // 16),
        cost_estimate=pl.CostEstimate(flops=0, bytes_accessed=4 * depth * wide, transcendentals=0),
    )(block)


def call(kernel, *, high, sum_width, specs, arrays, blocks, out_shape, scratch=()):
    n = len(blocks)
    depth = sum(b.shape[0] for b in blocks)
    rows, wide = arrays[0].shape[0], sum_width
    vmem = pl.BlockSpec(memory_space=pltpu.VMEM)
    return pl.pallas_call(
        functools.partial(kernel, functools.partial(add_blocks, specs, high), n),
        out_shape=out_shape,
        in_specs=[vmem] * (len(arrays) + n),
        out_specs=jax.tree.map(lambda _: vmem, out_shape),
        scratch_shapes=list(scratch),
        compiler_params=pltpu.CompilerParams(vmem_limit_bytes=vmem_bytes),
        cost_estimate=pl.CostEstimate(
            flops=4 * rows * depth * wide, bytes_accessed=2 * depth * wide + 16 * rows * wide, transcendentals=0
        ),
    )(*arrays, *blocks)


def make_on_device(count):
    high = count // 4

    def move(where):
        pairs = []
        for f in range(count):
            y, x, c = where(f // 4, (f // 2) % 2, f % 2)
            pairs.append((f, (y % high) * 4 + (x % 2) * 2 + c % 2))
        return lambda v: lax.ppermute(v, "fsdp", pairs)

    along = move(lambda y, x, c: (y + 1 - 2 * c, x, c))
    across = move(lambda y, x, c: (y, x + 1, c))
    swap = move(lambda y, x, c: (y, x, c + 1))
    core_pairs = [[f, f + 1] for f in range(0, count, 2)]

    def join(v):
        return lax.all_gather(v, "fsdp", axis=0, tiled=True, axis_index_groups=core_pairs)

    def on_device(tokens, norm_gain, gate_weight, up_weight):
        gain = norm_gain[:, None]
        own = jnp.concatenate([gate_weight * gain, up_weight * gain], axis=1).astype(jnp.bfloat16)
        wide = own.shape[1]
        b0 = across(own)
        chip, late = lax.optimization_barrier((join(own), tokens))
        rows = tokens.shape[0]
        sums = jax.ShapeDtypeStruct((rows, wide), jnp.float32)
        step = functools.partial(call, high=high, sum_width=wide)

        a1 = along(chip)
        b1 = along(join(b0))
        others = swap(late)
        a2 = along(a1)
        b2 = along(b1)
        a3 = along(cut(a2))
        a3_rest = along(cut(a2, 1))
        total, partial, scale = step(
            first_kernel,
            specs=[(0, 0, 1), (1, 0, 0), (1, 1, 0), (2, 0, 0)],
            arrays=[tokens, others],
            blocks=[own, a1, b1, a2],
            out_shape=(sums, sums, jax.ShapeDtypeStruct((rows, 1), jnp.float32)),
        )
        b2, total = lax.optimization_barrier((b2, total))
        b3 = along(cut(b2))
        b3_rest = along(cut(b2, 1))
        a4 = along(a3)
        narrow = jax.ShapeDtypeStruct((rows, wide // 2), jnp.float32)
        total, gate, up = step(
            second_kernel,
            specs=[(0, 1, 1), (2, 1, 0), (3, 0, 1), (3, 0, 2)],
            arrays=[tokens, others, total, partial],
            blocks=[b0, b2, a3, a3_rest],
            out_shape=(sums, narrow, narrow),
            scratch=[pltpu.VMEM((rows, wide), jnp.float32)],
        )
        b3, total = lax.optimization_barrier((b3, total))
        b4 = along(b3)
        total, late = step(
            third_kernel,
            specs=[(3, 1, 1), (3, 1, 2), (4, 0, 1)],
            arrays=[tokens, others, total, join(gate), join(up)],
            blocks=[b3, b3_rest, a4],
            out_shape=(sums, jax.ShapeDtypeStruct((rows, wide), jnp.bfloat16)),
            scratch=[pltpu.VMEM((rows, wide), jnp.float32)],
        )
        late_joined = join(late)
        return step(
            last_kernel,
            specs=[(4, 1, 0)],
            arrays=[tokens, total, late_joined, scale],
            blocks=[join(b4)],
            out_shape=jax.ShapeDtypeStruct((rows, wide // 2), jnp.bfloat16),
            scratch=[pltpu.VMEM((rows, wide), jnp.float32)],
        )

    return on_device


def solution(mesh):
    return jax.shard_map(
        make_on_device(mesh.shape["fsdp"]),
        mesh=mesh,
        in_specs=(P("fsdp", None), P("fsdp"), P("fsdp", "tensor"), P("fsdp", "tensor")),
        out_specs=P("fsdp", "tensor"),
        check_vma=False,
    )
```

```python
import functools

import jax
import jax.numpy as jnp
from jax import lax
from jax.experimental import pallas as pl
from jax.experimental.pallas import tpu as pltpu
from jax.sharding import PartitionSpec as P

epsilon = 1e-05
vmem_bytes = 16 * 1024 * 1024


def column(spec, high):
    steps, other, half = spec
    index = lax.axis_index("fsdp")
    core = lax.rem(index, 2)
    x = lax.rem(lax.div(index, 2), 2)
    y = lax.rem(lax.div(index, 4) + (steps * (2 * core - 1) + high), high)
    return (y * 2 + (1 - x if other else x)) * 2 + (0, core, 1 - core)[half]


def add_blocks(specs, high, blocks, pairs):
    for spec, block in zip(specs, blocks):
        depth = block.shape[0]
        unit = depth if spec[2] else depth // 2
        start = pl.multiple_of(column(spec, high) * unit, unit)
        for tokens, total in pairs:
            total[...] += jnp.dot(tokens[:, pl.ds(start, depth)], block[...], preferred_element_type=jnp.float32)


def first_kernel(add, n, tokens, others, *refs):
    blocks, (total, partial, scale) = refs[:n], refs[n:]
    values = tokens[...].astype(jnp.float32)
    scale[...] = lax.rsqrt(jnp.mean(values * values, axis=1, keepdims=True) + epsilon)
    total[...] = jnp.zeros_like(total)
    partial[...] = jnp.zeros_like(partial)
    add(blocks, [(tokens, total), (others, partial)])


def second_kernel(add, n, tokens, others, total_before, partial_before, *refs):
    blocks, (total, gate, up, partial) = refs[:n], refs[n:]
    total[...] = total_before[...]
    partial[...] = partial_before[...]
    add(blocks, [(tokens, total), (others, partial)])
    wide = gate.shape[1]
    gate[...] = partial[:, :wide]
    up[...] = partial[:, wide:]


def their_rows(rows):
    return pl.ds(pl.multiple_of((1 - lax.rem(lax.axis_index("fsdp"), 2)) * rows, rows), rows)


def third_kernel(add, n, tokens, others, total_before, gate_arrived, up_arrived, *refs):
    blocks, (total, partial) = refs[:n], refs[n:]
    wide = gate_arrived.shape[1]
    theirs = their_rows(total.shape[0])
    total[:, :wide] = total_before[:, :wide] + gate_arrived[theirs, :]
    total[:, wide:] = total_before[:, wide:] + up_arrived[theirs, :]
    partial[...] = jnp.zeros_like(partial)
    add(blocks, [(tokens, total), (others, partial)])


def fourth_kernel(add, n, tokens, others, total_before, partial_before, *refs):
    blocks, (total, leaving, partial) = refs[:n], refs[n:]
    total[...] = total_before[...]
    partial[...] = partial_before[...]
    add(blocks, [(tokens, total), (others, partial)])
    leaving[...] = partial[...].astype(leaving.dtype)


def last_kernel(add, n, total, late, scale, hidden):
    rows, wide = hidden.shape
    theirs = their_rows(rows)
    gate = (total[:, :wide] + late[theirs, :wide].astype(jnp.float32)) * scale[...]
    up = (total[:, wide:] + late[theirs, wide:].astype(jnp.float32)) * scale[...]
    hidden[...] = (gate / (1.0 + jnp.exp(-gate)) * up).astype(hidden.dtype)


def gain_kernel(gain, gate, up, own):
    depth, wide = gate.shape
    shape = (depth, depth)
    here = lax.broadcasted_iota(jnp.int32, shape, 0) == lax.broadcasted_iota(jnp.int32, shape, 1)
    column = jnp.sum(jnp.where(here, gain[...], 0.0), axis=1, keepdims=True)
    own[:, :wide] = (gate[...].astype(jnp.float32) * column).astype(own.dtype)
    own[:, wide:] = (up[...].astype(jnp.float32) * column).astype(own.dtype)


def cut_kernel(flip, depth, block, out, sem):
    start = pl.multiple_of(lax.rem(lax.axis_index("fsdp") + flip, 2) * depth, depth)
    copy = pltpu.make_async_copy(block.at[pl.ds(start, depth)], out, sem)
    copy.start()
    copy.wait()


def cut(block, flip=0):
    depth, wide = block.shape[0] // 2, block.shape[1]
    anywhere = pl.BlockSpec(memory_space=pl.ANY)
    return pl.pallas_call(
        functools.partial(cut_kernel, flip, depth),
        out_shape=jax.ShapeDtypeStruct((depth, wide), block.dtype),
        in_specs=[anywhere],
        out_specs=anywhere,
        scratch_shapes=[pltpu.SemaphoreType.DMA],
        compiler_params=pltpu.CompilerParams(vmem_limit_bytes=vmem_bytes // 16),
        cost_estimate=pl.CostEstimate(flops=0, bytes_accessed=4 * depth * wide, transcendentals=0),
    )(block)


def call(kernel, *, high, sum_width, specs, arrays, blocks, out_shape, scratch=()):
    n = len(blocks)
    depth = sum(b.shape[0] for b in blocks)
    rows, wide = arrays[0].shape[0], sum_width
    vmem = pl.BlockSpec(memory_space=pltpu.VMEM)
    return pl.pallas_call(
        functools.partial(kernel, functools.partial(add_blocks, specs, high), n),
        out_shape=out_shape,
        in_specs=[vmem] * (len(arrays) + n),
        out_specs=jax.tree.map(lambda _: vmem, out_shape),
        scratch_shapes=list(scratch),
        compiler_params=pltpu.CompilerParams(vmem_limit_bytes=vmem_bytes),
        cost_estimate=pl.CostEstimate(
            flops=4 * rows * depth * wide, bytes_accessed=2 * depth * wide + 16 * rows * wide, transcendentals=0
        ),
    )(*arrays, *blocks)


def make_on_device(count):
    high = count // 4

    def move(where):
        pairs = []
        for f in range(count):
            y, x, c = where(f // 4, (f // 2) % 2, f % 2)
            pairs.append((f, (y % high) * 4 + (x % 2) * 2 + c % 2))
        return lambda v: lax.ppermute(v, "fsdp", pairs)

    along = move(lambda y, x, c: (y + 1 - 2 * c, x, c))
    across = move(lambda y, x, c: (y, x + 1, c))
    swap = move(lambda y, x, c: (y, x, c + 1))
    core_pairs = [[f, f + 1] for f in range(0, count, 2)]

    def join(v):
        return lax.all_gather(v, "fsdp", axis=0, tiled=True, axis_index_groups=core_pairs)

    def on_device(tokens, norm_gain, gate_weight, up_weight):
        vmem = pl.BlockSpec(memory_space=pltpu.VMEM)
        own = pl.pallas_call(
            gain_kernel,
            out_shape=jax.ShapeDtypeStruct((gate_weight.shape[0], 2 * gate_weight.shape[1]), jnp.bfloat16),
            in_specs=[vmem] * 3,
            out_specs=vmem,
            compiler_params=pltpu.CompilerParams(vmem_limit_bytes=vmem_bytes // 4),
        )(norm_gain[None, :], gate_weight, up_weight)
        wide = own.shape[1]
        b0 = across(own)
        chip, late = lax.optimization_barrier((join(own), tokens))
        rows = tokens.shape[0]
        sums = jax.ShapeDtypeStruct((rows, wide), jnp.float32)
        step = functools.partial(call, high=high, sum_width=wide)

        a1 = along(chip)
        b1 = along(join(b0))
        others = swap(late)
        a2 = along(a1)
        b2 = along(b1)
        a3 = along(cut(a2))
        a3_rest = along(cut(a2, 1))
        total, partial, scale = step(
            first_kernel,
            specs=[(0, 0, 1), (1, 0, 0), (1, 1, 0), (2, 0, 0)],
            arrays=[tokens, others],
            blocks=[own, a1, b1, a2],
            out_shape=(sums, sums, jax.ShapeDtypeStruct((rows, 1), jnp.float32)),
        )
        b2, total = lax.optimization_barrier((b2, total))
        b3 = along(cut(b2))
        b3_rest = along(cut(b2, 1))
        a4 = along(a3)
        narrow = jax.ShapeDtypeStruct((rows, wide // 2), jnp.float32)
        total, gate, up = step(
            second_kernel,
            specs=[(0, 1, 1), (2, 1, 0), (3, 0, 1), (3, 0, 2)],
            arrays=[tokens, others, total, partial],
            blocks=[b0, b2, a3, a3_rest],
            out_shape=(sums, narrow, narrow),
            scratch=[pltpu.VMEM((rows, wide), jnp.float32)],
        )
        b3, total = lax.optimization_barrier((b3, total))
        b4 = along(b3)
        total, partial = step(
            third_kernel,
            specs=[(3, 1, 1), (3, 1, 2), (4, 0, 1)],
            arrays=[tokens, others, total, join(gate), join(up)],
            blocks=[b3, b3_rest, a4],
            out_shape=(sums, sums),
        )
        b4, total = lax.optimization_barrier((b4, total))
        total, late = step(
            fourth_kernel,
            specs=[(4, 1, 1)],
            arrays=[tokens, others, total, partial],
            blocks=[b4],
            out_shape=(sums, jax.ShapeDtypeStruct((rows, wide), jnp.bfloat16)),
            scratch=[pltpu.VMEM((rows, wide), jnp.float32)],
        )
        return step(
            last_kernel,
            specs=[],
            arrays=[total, join(late), scale],
            blocks=[],
            out_shape=jax.ShapeDtypeStruct((rows, wide // 2), jnp.bfloat16),
        )

    return on_device


def solution(mesh):
    return jax.shard_map(
        make_on_device(mesh.shape["fsdp"]),
        mesh=mesh,
        in_specs=(P("fsdp", None), P("fsdp"), P("fsdp", "tensor"), P("fsdp", "tensor")),
        out_specs=P("fsdp", "tensor"),
        check_vma=False,
    )
```
